256 devices in a mesh: gy: 16 (over z, core), gz: 16 (over x, y).
Axes of the slice: x: 4, y: 4, z: 8, core: 2. Of those that a mesh axis runs over, the one named last changes fastest.
Arguments:
- state_field: bfloat16 [11, 256, 512, 512], P(None, 'gz', 'gy'), may hold values from -100 to 100, as said below
- start_factor: float32 [512, 64], replicated, may hold values from -6 to 6
Outputs:
- factor_one: float32 [512, 64], replicated
- mode_two_gram: float32 [512, 512], P('gy')
The draws below stay inside these ranges and needn't reach their ends.
Inputs may be any that keep to these rules, and one draw needn't show every extreme that they name: `state_field`: Real-valued field of full rank along every mode.
All inputs are finite; a program needn't handle non-finite values.
Results may differ from the reference program's by a relative error of at most 0.00052.
Values may be sent and summed in bfloat16 or wider, within the bound.
No kernel may reach another device: no remote copies, remote signals or barrier semaphores. Data moves between devices by JAX's collectives and lax.ppermute only.
A program may use at most 64 MiB of HBM per device.

```python
import math
import jax
import jax.numpy as jnp
from jax import lax

N1 = 512
NV = 11
R1 = 64
ITERS = 6
N2 = 512
N3 = 256


def draw_state_field(key, part):
    keys = jax.random.split(key, 5)
    shape = (NV, N3, N2, N1)
    noise = jnp.clip(jax.random.normal(keys[0], shape, jnp.float32), -6.0, 6.0)
    ranks = jax.random.permutation(keys[1], N1).astype(jnp.float32)
    decay = 10.0 ** (-ranks / N1)
    depth_scale = jnp.exp(jax.random.uniform(keys[2], (N3,), jnp.float32, math.log(0.3), math.log(3.0)))
    cross_scale = jnp.exp(jax.random.uniform(keys[4], (N2,), jnp.float32, math.log(0.3), math.log(3.0)))
    base = noise * decay * cross_scale[:, None] * depth_scale[:, None, None]
    mixer = jax.random.permutation(keys[3], N1)
    return (base + 0.7 * jnp.take(base, mixer, axis=3)).astype(jnp.bfloat16)


def normal_values(own_key, extent, scale, reach, held_as=jnp.bfloat16):
    drawn = scale * jax.random.normal(own_key, extent, jnp.float32)
    return jnp.clip(drawn, min=-reach, max=reach).astype(held_as)


def setup_inputs(seed: int = 0) -> dict:
    splits = jax.random.split(jax.random.key(seed), 3)
    return {
        "state_field": draw_state_field(jax.random.fold_in(splits[2], 71), 0),
        "start_factor": normal_values(splits[1], (N1, R1), 1.0, 6.0, jnp.float32),
    }


def orthonormalize(images):
    cross_gram = jnp.dot(images.T, images, precision=lax.Precision.HIGHEST)
    lower_tri = jnp.linalg.cholesky(cross_gram)
    return lax.linalg.triangular_solve(lower_tri, images, left_side=False, lower=True, transpose_a=True)

def reference(state_field, start_factor):
    mode_gram = jnp.zeros((N1, N1), jnp.float32)
    for variable in range(NV):
        flattened = state_field[variable].astype(jnp.float32).reshape(-1, N1)
        mode_gram = mode_gram + lax.dot_general(flattened, flattened, (((0,), (0,)), ((), ())), precision=lax.Precision.HIGHEST)
    factor_one = start_factor
    for iteration in range(ITERS):
        images = jnp.dot(mode_gram, factor_one, precision=lax.Precision.HIGHEST)
        factor_one = orthonormalize(images)
    narrow = factor_one.astype(jnp.bfloat16).astype(jnp.float32)
    second = jnp.zeros((N2, N2), jnp.float32)
    for variable in range(NV):
        slab = state_field[variable].astype(jnp.float32)
        shrunk = jnp.einsum('kji,ir->jkr', slab, narrow, precision=lax.Precision.HIGHEST).astype(jnp.bfloat16)
        matrix = shrunk.astype(jnp.float32).reshape(N2, -1)
        second = second + lax.dot_general(matrix, matrix, (((1,), (1,)), ((), ())), precision=lax.Precision.HIGHEST)
    return (factor_one, second / (NV * N3 * R1))
```

```python
import jax
import jax.numpy as jnp
from jax import lax
from jax.sharding import Mesh, PartitionSpec as P

ITERS = 6
Z, C, X, Y = 8, 2, 4, 4
B = 128
SWAP = [(0, 1), (1, 0)]


def orthonormalize(images):
    cross_gram = jnp.dot(images.T, images, precision=lax.Precision.HIGHEST)
    lower_tri = jnp.linalg.cholesky(cross_gram)
    return lax.linalg.triangular_solve(
        lower_tri, images, left_side=False, lower=True, transpose_a=True
    )


def exchange(pieces, axes):
    return lax.all_to_all(pieces, axes, 0, 0)


def to_all(piece, axes, count):
    return exchange(jnp.broadcast_to(piece[None], (count,) + piece.shape), axes)


def sum_gram(partial):
    core = lax.axis_index("c")
    tiles = partial.shape[0] // B
    pairs = [(a, b) for a in range(tiles) for b in range(a, tiles)]
    half = len(pairs) // 2
    packed = jnp.stack([partial[a * B:(a + 1) * B, b * B:(b + 1) * B] for a, b in pairs])
    mine = lax.dynamic_slice_in_dim(packed, core * half, half)
    other = lax.dynamic_slice_in_dim(packed, (1 - core) * half, half)
    mine = mine + lax.ppermute(other, "c", SWAP)
    piece = exchange(mine.reshape(X * Y, -1, B), ("x", "y")).sum(0)
    piece = to_all(piece, "z", Z).sum(0)
    mine = to_all(piece, ("x", "y"), X * Y).reshape(half, B, B)
    other = lax.ppermute(mine, "c", SWAP)
    first = jnp.where(core == 0, mine, other)
    last = jnp.where(core == 0, other, mine)
    block = {}
    for place, (a, b) in enumerate(pairs):
        block[a, b] = first[place] if place < half else last[place - half]
        if a != b:
            block[b, a] = block[a, b].T
    return jnp.block([[block[a, b] for b in range(tiles)] for a in range(tiles)])


def per_device(state_field, start_factor):
    variables, depth, rows, mode_one = state_field.shape
    flattened = state_field.reshape(-1, mode_one)
    partial_value = lax.dot_general(
        flattened, flattened, (((0,), (0,)), ((), ())), preferred_element_type=jnp.float32
    )
    mode_gram = sum_gram(partial_value)
    factor_one = start_factor
    for iteration in range(ITERS):
        images = jnp.dot(mode_gram, factor_one, precision=lax.Precision.HIGHEST)
        factor_one = orthonormalize(images)
    narrow = factor_one.astype(jnp.bfloat16)
    rank = narrow.shape[1]
    shrunk = jnp.einsum(
        "vkji,ir->kjvr", state_field, narrow, preferred_element_type=jnp.float32
    ).astype(jnp.bfloat16)
    matrix = exchange(shrunk.reshape(depth, rows, variables * rank), ("z", "c"))
    matrix = matrix.reshape(-1, variables * rank)
    partial_two = lax.dot_general(
        matrix, matrix, (((1,), (1,)), ((), ())), preferred_element_type=jnp.float32
    )
    core = lax.axis_index("c")
    split = partial_two.reshape(Z, C, -1, B)
    mine = lax.dynamic_index_in_dim(split, core, 1, keepdims=False)
    other = lax.dynamic_index_in_dim(split, 1 - core, 1, keepdims=False)
    mine = mine + lax.ppermute(other, "c", SWAP)
    piece = exchange(mine, "z").sum(0)
    second = to_all(piece, ("x", "y"), X * Y).sum(0)
    second = second.reshape(rows, -1)
    divisor = variables * depth * X * Y * rank
    return (factor_one, second / divisor)


def solution(mesh):
    fine = Mesh(mesh.devices.reshape(Z, C, X, Y), ("z", "c", "x", "y"))
    placed = (P(None, ("x", "y"), ("z", "c"), None), P())
    return jax.shard_map(
        per_device, mesh=fine, in_specs=placed, out_specs=(P(), P(("z", "c"), None)), check_vma=False
    )
```

```python
import jax
import jax.numpy as jnp
from jax import lax
from jax.experimental import pallas as pl
from jax.experimental.pallas import tpu as pltpu
from jax.sharding import Mesh, PartitionSpec as P

ITERS = 6
Z, C, X, Y = 8, 2, 4, 4
B = 128
SWAP = [(0, 1), (1, 0)]
TN = (((0,), (0,)), ((), ()))
NT = (((1,), (1,)), ((), ()))
f32, bf16 = jnp.float32, jnp.bfloat16
vmem = pl.BlockSpec(memory_space=pltpu.VMEM)
smem = pl.BlockSpec(memory_space=pltpu.SMEM)


def upper_pairs(tiles):
    return [(a, b) for a in range(tiles) for b in range(a, tiles)]


def gram_kernel(core_ref, x_ref, mine_ref, other_ref, upper, lower):
    step = pl.program_id(0)
    h = lower.shape[0]
    x = x_ref[...]
    one = lax.dot_general(x[:, :h], x, TN, preferred_element_type=f32)
    two = lax.dot_general(x[:, h:], x[:, h:], TN, preferred_element_type=f32)

    @pl.when(step == 0)
    def _():
        upper[...] = one
        lower[...] = two

    @pl.when(step > 0)
    def _():
        upper[...] += one
        lower[...] += two

    pairs = upper_pairs(upper.shape[1] // B)
    half = len(pairs) // 2

    def write(first_ref, last_ref):
        for place, (a, b) in enumerate(pairs):
            ref = first_ref if place < half else last_ref
            if a * B < h:
                block = upper[a * B:(a + 1) * B, b * B:(b + 1) * B]
            else:
                block = lower[a * B - h:(a + 1) * B - h, b * B - h:(b + 1) * B - h]
            ref[place % half] = block

    last = step == pl.num_programs(0) - 1
    pl.when(last & (core_ref[0] == 0))(lambda: write(mine_ref, other_ref))
    pl.when(last & (core_ref[0] == 1))(lambda: write(other_ref, mine_ref))


def partial_gram(core, x):
    total, n = x.shape
    half = len(upper_pairs(n // B)) // 2
    out = jax.ShapeDtypeStruct((half, B, B), f32)
    whole = pl.BlockSpec((half, B, B), lambda i: (0, 0, 0))
    return pl.pallas_call(
        gram_kernel,
        grid=(2,),
        in_specs=[smem, pl.BlockSpec((total // 2, n), lambda i: (i, 0))],
        out_specs=(whole, whole),
        out_shape=(out, out),
        scratch_shapes=[pltpu.VMEM((n // 2, n), f32), pltpu.VMEM((n // 2, n // 2), f32)],
        compiler_params=pltpu.CompilerParams(vmem_limit_bytes=40 * 2**20),
        name="partial_gram",
    )(core, x)


def split3(x):
    high = x.astype(bf16)
    rest = x - high.astype(f32)
    mid = rest.astype(bf16)
    return high, mid, (rest - mid.astype(f32)).astype(bf16)


def dot(a, b):
    return jnp.dot(a, b, preferred_element_type=f32)


def product(left, right):
    n = left[0].shape[0]
    one = dot(jnp.concatenate(left, 0), right[0])
    two = dot(jnp.concatenate(left[:2], 0), right[1])
    three = dot(left[0], right[2])
    return one[:n] + (one[n:2 * n] + two[:n] + (one[2 * n:] + two[n:] + three))


def gram_of_rows(parts):
    n = parts[0].shape[0]
    stacked = jnp.concatenate(parts, 0)
    full = lax.dot_general(stacked, stacked, NT, preferred_element_type=f32)

    def part(i, j):
        return full[i * n:(i + 1) * n, j * n:(j + 1) * n]

    return part(0, 0) + ((part(0, 1) + part(1, 0)) + (part(1, 1) + part(0, 2) + part(2, 0)))


def reciprocal(d):
    r = pl.reciprocal(d, approx=True)
    r = r * (2.0 - d * r)
    return r * (2.0 - d * r)


def inverse_factor(a, panel=8):
    n = a.shape[0]
    row = lax.broadcasted_iota(jnp.int32, (n, n), 0)
    lane = lax.broadcasted_iota(jnp.int32, (n, n), 1)
    work = jnp.concatenate([a, jnp.where(row == lane, 1.0, 0.0)], 1)
    finished, pivots = [], []
    for start in range(0, n, panel):
        here = lax.broadcasted_iota(jnp.int32, work.shape, 0)
        columns = [
            jnp.broadcast_to(work[:, start + c:start + c + 1], work.shape) for c in range(panel)
        ]
        for j in range(panel):
            pivot = columns[j][j:j + 1]
            pivots.append(pivot)
            factor = jnp.where(here > j, columns[j] * reciprocal(pivot), 0.0)
            for c in range(j + 1, panel):
                columns[c] = columns[c] - factor * columns[c][j:j + 1]
            work = work - factor * work[j:j + 1]
        finished.append(work[:panel])
        work = work[panel:]
    scale = lax.rsqrt(jnp.concatenate(pivots, 0))
    return (jnp.concatenate(finished, 0) * scale)[:, n:]


def factor_kernel(core_ref, x_hbm, mine_ref, other_ref, start_ref, factor_ref, shrunk_ref, g1, g2, g3, x_ref, sem):
    copy = pltpu.make_async_copy(x_hbm, x_ref, sem)
    copy.start()
    pairs = upper_pairs(g1.shape[0] // B)
    half = len(pairs) // 2
    even = core_ref[0] == 0
    for place, (a, b) in enumerate(pairs):
        mine, other = mine_ref[place % half], other_ref[place % half]
        block = jnp.where(even, mine, other) if place < half else jnp.where(even, other, mine)
        for i, j in ((a, b), (b, a))[:1 if a == b else 2]:
            for ref, part in zip((g1, g2, g3), split3(block if i == a else block.T)):
                ref[i * B:(i + 1) * B, j * B:(j + 1) * B] = part

    def times_gram(parts):
        return product(parts, (g1[...], g2[...], g3[...]))

    def iteration(_, images):
        parts = split3(images)
        inverse = inverse_factor(gram_of_rows(parts))
        return product(split3(inverse), split3(times_gram(parts)))

    images = lax.fori_loop(0, ITERS - 1, iteration, times_gram(split3(start_ref[...])))
    parts = split3(images)
    factor = product(split3(inverse_factor(gram_of_rows(parts))), parts)
    factor_ref[...] = factor

    narrow = factor.T.astype(bf16)
    n, rank = narrow.shape
    blank = jnp.zeros_like(narrow)
    both = jnp.concatenate(
        [jnp.concatenate([narrow, blank], 1), jnp.concatenate([blank, narrow], 1)], 0
    )
    variables, depth, rows, _ = x_ref.shape
    chunk = depth // 2
    copy.wait()

    def shrink(t, _):
        k = pl.ds(t * chunk, chunk)
        for v in range(0, variables, 2):
            x = x_ref[v, k].reshape(-1, n)
            if v + 1 < variables:
                out = dot(jnp.concatenate([x, x_ref[v + 1, k].reshape(-1, n)], 1), both)
            else:
                out = dot(x, narrow)
            width = out.shape[1]
            shrunk_ref[k, :, v * rank:v * rank + width] = out.astype(bf16).reshape(chunk, rows, width)
        return 0

    lax.fori_loop(0, depth // chunk, shrink, 0)


def factor_and_shrink(core, x, mine, other, start_factor):
    n, rank = start_factor.shape
    variables, depth, rows, _ = x.shape
    factor, shrunk = pl.pallas_call(
        factor_kernel,
        in_specs=[smem, pl.BlockSpec(memory_space=pl.ANY), vmem, vmem, vmem],
        out_specs=(vmem, vmem),
        out_shape=(
            jax.ShapeDtypeStruct((rank, n), f32),
            jax.ShapeDtypeStruct((depth, rows, variables * rank), bf16),
        ),
        scratch_shapes=[pltpu.VMEM((n, n), bf16)] * 3
        + [pltpu.VMEM(x.shape, bf16), pltpu.SemaphoreType.DMA(())],
        compiler_params=pltpu.CompilerParams(vmem_limit_bytes=40 * 2**20),
        name="factor_and_shrink",
    )(core, x, mine, other, start_factor.T)
    return factor.T, shrunk


def exchange(pieces, axes):
    return lax.all_to_all(pieces, axes, 0, 0)


def to_all(piece, axes, count):
    return exchange(jnp.broadcast_to(piece[None], (count,) + piece.shape), axes)


def per_device(state_field, start_factor):
    variables, depth, rows, mode_one = state_field.shape
    rank = start_factor.shape[1]
    index = lax.axis_index("c")
    core = index.astype(jnp.int32)[None]

    mine, other = partial_gram(core, state_field.reshape(-1, mode_one))
    mine = mine + lax.ppermute(other, "c", SWAP)
    piece = exchange(mine.reshape(X * Y, -1, B), ("x", "y")).sum(0)
    piece = to_all(piece, "z", Z).sum(0)
    mine = to_all(piece, ("x", "y"), X * Y).reshape(mine.shape)
    other = lax.ppermute(mine, "c", SWAP)

    factor_one, shrunk = factor_and_shrink(core, state_field, mine, other, start_factor)

    matrix = exchange(shrunk, ("z", "c")).reshape(-1, variables * rank)
    partial_two = lax.dot_general(matrix, matrix, NT, preferred_element_type=f32)
    divided = partial_two.reshape(Z, C, rows, -1)
    mine = lax.dynamic_index_in_dim(divided, index, 1, keepdims=False)
    other = lax.dynamic_index_in_dim(divided, 1 - index, 1, keepdims=False)
    mine = mine + lax.ppermute(other, "c", SWAP)
    piece = exchange(mine, "z").sum(0)
    second = to_all(piece, ("x", "y"), X * Y).sum(0)
    divisor = variables * depth * X * Y * rank
    return (factor_one, second / divisor)


def solution(mesh):
    fine = Mesh(mesh.devices.reshape(Z, C, X, Y), ("z", "c", "x", "y"))
    placed = (P(None, ("x", "y"), ("z", "c"), None), P())
    return jax.shard_map(
        per_device, mesh=fine, in_specs=placed, out_specs=(P(), P(("z", "c"), None)), check_vma=False
    )
```

```python
import functools

import jax
import jax.numpy as jnp
from jax import lax
from jax.experimental import pallas as pl
from jax.experimental.pallas import tpu as pltpu
from jax.sharding import Mesh, PartitionSpec as P

ITERS = 6
Z, C, X, Y = 8, 2, 4, 4
B = 128
SWAP = [(0, 1), (1, 0)]
TN = (((0,), (0,)), ((), ()))
NT = (((1,), (1,)), ((), ()))
f32, bf16 = jnp.float32, jnp.bfloat16
vmem = pl.BlockSpec(memory_space=pltpu.VMEM)
smem = pl.BlockSpec(memory_space=pltpu.SMEM)
hbm = pl.BlockSpec(memory_space=pltpu.HBM)


def upper_pairs(tiles):
    return [(a, b) for a in range(tiles) for b in range(a, tiles)]


def gram_kernel(chunks, core_ref, x_hbm, mine_ref, other_ref, x_ref, upper, lower, sems):
    starts = [sum(chunks[:i]) for i in range(len(chunks))]
    copies = [
        pltpu.make_async_copy(x_hbm.at[pl.ds(at, size)], x_ref.at[pl.ds(at, size)], sems.at[i])
        for i, (at, size) in enumerate(zip(starts, chunks))
    ]
    for copy in copies:
        copy.start()
    h = lower.shape[0]
    for i, (at, size) in enumerate(zip(starts, chunks)):
        copies[i].wait()
        x = x_ref[pl.ds(at, size)]
        one = lax.dot_general(x[:, :h], x, TN, preferred_element_type=f32)
        two = lax.dot_general(x[:, h:], x[:, h:], TN, preferred_element_type=f32)
        if i:
            one, two = one + upper[...], two + lower[...]
        upper[...], lower[...] = one, two

    pairs = upper_pairs(upper.shape[1] // B)
    half = len(pairs) // 2

    def write(first_ref, last_ref):
        for place, (a, b) in enumerate(pairs):
            ref = first_ref if place < half else last_ref
            if a * B < h:
                block = upper[a * B:(a + 1) * B, b * B:(b + 1) * B]
            else:
                block = lower[a * B - h:(a + 1) * B - h, b * B - h:(b + 1) * B - h]
            ref[place % half] = block

    pl.when(core_ref[0] == 0)(lambda: write(mine_ref, other_ref))
    pl.when(core_ref[0] == 1)(lambda: write(other_ref, mine_ref))


def partial_gram(core, x):
    total, n = x.shape
    half = len(upper_pairs(n // B)) // 2
    out = jax.ShapeDtypeStruct((half, B, B), f32)
    chunks = (total // 11 * 3, total // 11 * 4, total // 11 * 4)
    return pl.pallas_call(
        functools.partial(gram_kernel, chunks),
        in_specs=[smem, hbm],
        out_specs=(vmem, vmem),
        out_shape=(out, out),
        scratch_shapes=[
            pltpu.VMEM((total, n), bf16),
            pltpu.VMEM((n // 2, n), f32),
            pltpu.VMEM((n // 2, n // 2), f32),
            pltpu.SemaphoreType.DMA((len(chunks),)),
        ],
        compiler_params=pltpu.CompilerParams(vmem_limit_bytes=50 * 2**20),
        name="partial_gram",
    )(core, x)


def split3(x):
    high = x.astype(bf16)
    rest = x - high.astype(f32)
    mid = rest.astype(bf16)
    return high, mid, (rest - mid.astype(f32)).astype(bf16)


def dot(a, b):
    return jnp.dot(a, b, preferred_element_type=f32)


def product(left, right):
    n = left[0].shape[0]
    one = dot(jnp.concatenate(left, 0), right[0])
    two = dot(jnp.concatenate(left[:2], 0), right[1])
    three = dot(left[0], right[2])
    return one[:n] + (one[n:2 * n] + two[:n] + (one[2 * n:] + two[n:] + three))


def gram_of_rows(parts):
    n = parts[0].shape[0]
    stacked = jnp.concatenate(parts, 0)
    full = lax.dot_general(stacked, stacked, NT, preferred_element_type=f32)

    def part(i, j):
        return full[i * n:(i + 1) * n, j * n:(j + 1) * n]

    return part(0, 0) + ((part(0, 1) + part(1, 0)) + (part(1, 1) + part(0, 2) + part(2, 0)))


def reciprocal(d):
    r = pl.reciprocal(d, approx=True)
    return r * (2.0 - d * r)


def inverse_factor(a):
    n = a.shape[0]
    row = lax.broadcasted_iota(jnp.int32, (n, n), 0)
    lane = lax.broadcasted_iota(jnp.int32, (n, n), 1)
    work = jnp.concatenate([a, jnp.where(row == lane, 1.0, 0.0)], 1)
    finished, pivots = [], []
    start = 0
    for panel in (16,) * 4:
        here = lax.broadcasted_iota(jnp.int32, work.shape, 0)
        columns = [
            jnp.broadcast_to(work[:, start + c:start + c + 1], work.shape) for c in range(panel)
        ]
        for j in range(0, panel, 2):
            u, v = columns[j], columns[j + 1]
            p, q, r = u[j:j + 1], u[j + 1:j + 2], v[j + 1:j + 2]
            over = reciprocal(p * r - q * q)
            below = here > j + 1
            one = jnp.where(below, (r * u - q * v) * over, 0.0)
            two = jnp.where(below, (p * v - q * u) * over, 0.0)
            for c in range(j + 2, panel):
                column = columns[c]
                columns[c] = column - (one * column[j:j + 1] + two * column[j + 1:j + 2])
            ratio = q * reciprocal(p)
            pivots += [p, r - q * ratio]
            one = jnp.where(here == j + 1, ratio, one)
            work = work - (one * work[j:j + 1] + two * work[j + 1:j + 2])
        finished.append(work[:panel])
        work = work[panel:]
        start += panel
    scale = lax.rsqrt(jnp.concatenate(pivots, 0))
    return (jnp.concatenate(finished, 0) * scale)[:, n:]


def factor_kernel(core_ref, x_hbm, mine_ref, other_ref, start_ref, factor_ref, shrunk_ref, g1, g2, g3, x_ref, sem):
    copy = pltpu.make_async_copy(x_hbm, x_ref, sem)
    copy.start()
    pairs = upper_pairs(g1.shape[0] // B)
    half = len(pairs) // 2
    even = core_ref[0] == 0
    unit = lax.broadcasted_iota(jnp.int32, (B, B), 0) == lax.broadcasted_iota(jnp.int32, (B, B), 1)

    def packed(place):
        mine, other = mine_ref[place % half], other_ref[place % half]
        return jnp.where(even, mine, other) if place < half else jnp.where(even, other, mine)

    diagonal = sum(jnp.where(unit, packed(place), 0.0) for place, (a, b) in enumerate(pairs) if a == b)
    over_trace = 1.0 / jnp.sum(diagonal, keepdims=True)
    for place, (a, b) in enumerate(pairs):
        block = packed(place) * over_trace
        for i, j in ((a, b), (b, a))[:1 if a == b else 2]:
            for ref, part in zip((g1, g2, g3), split3(block if i == a else block.T)):
                ref[i * B:(i + 1) * B, j * B:(j + 1) * B] = part

    def times_gram(parts):
        return product(parts, (g1[...], g2[...], g3[...]))

    def iteration(_, images):
        parts = split3(images)
        inverse = inverse_factor(gram_of_rows(parts))
        return times_gram(split3(product(split3(inverse), parts)))

    images = lax.fori_loop(0, ITERS - 1, iteration, times_gram(split3(start_ref[...])))
    parts = split3(images)
    factor = product(split3(inverse_factor(gram_of_rows(parts))), parts)
    factor_ref[...] = factor

    narrow = factor.T.astype(bf16)
    n, rank = narrow.shape
    blank = jnp.zeros_like(narrow)
    both = jnp.concatenate(
        [jnp.concatenate([narrow, blank], 1), jnp.concatenate([blank, narrow], 1)], 0
    )
    variables, depth, rows, _ = x_ref.shape
    chunk = depth // 2
    copy.wait()

    def shrink(t, _):
        k = pl.ds(t * chunk, chunk)
        for v in range(0, variables, 2):
            x = x_ref[v, k].reshape(-1, n)
            if v + 1 < variables:
                out = dot(jnp.concatenate([x, x_ref[v + 1, k].reshape(-1, n)], 1), both)
            else:
                out = dot(x, narrow)
            width = out.shape[1]
            shrunk_ref[k, :, v * rank:v * rank + width] = out.astype(bf16).reshape(chunk, rows, width)
        return 0

    lax.fori_loop(0, depth // chunk, shrink, 0)


def factor_and_shrink(core, x, mine, other, start_factor):
    n, rank = start_factor.shape
    variables, depth, rows, _ = x.shape
    factor, shrunk = pl.pallas_call(
        factor_kernel,
        in_specs=[smem, hbm, vmem, vmem, vmem],
        out_specs=(vmem, vmem),
        out_shape=(
            jax.ShapeDtypeStruct((rank, n), f32),
            jax.ShapeDtypeStruct((depth, rows, variables * rank), bf16),
        ),
        scratch_shapes=[pltpu.VMEM((n, n), bf16)] * 3
        + [pltpu.VMEM(x.shape, bf16), pltpu.SemaphoreType.DMA(())],
        compiler_params=pltpu.CompilerParams(vmem_limit_bytes=50 * 2**20),
        name="factor_and_shrink",
    )(core, x, mine, other, start_factor.T)
    return factor.T, shrunk


def exchange(pieces, axes):
    return lax.all_to_all(pieces, axes, 0, 0)


def to_all(piece, axes, count):
    return exchange(jnp.broadcast_to(piece[None], (count,) + piece.shape), axes)


def per_device(state_field, start_factor):
    variables, depth, rows, mode_one = state_field.shape
    rank = start_factor.shape[1]
    index = lax.axis_index("c")
    core = index.astype(jnp.int32)[None]

    mine, other = partial_gram(core, state_field.reshape(-1, mode_one))
    mine = mine + lax.ppermute(other, "c", SWAP)
    piece = exchange(mine.reshape(X * Y, -1, B), ("x", "y")).sum(0)
    piece = to_all(piece, "z", Z).sum(0)
    mine = to_all(piece, ("x", "y"), X * Y).reshape(mine.shape)
    other = lax.ppermute(mine, "c", SWAP)

    factor_one, shrunk = factor_and_shrink(core, state_field, mine, other, start_factor)

    matrix = exchange(shrunk, ("z", "c")).reshape(-1, variables * rank)
    partial_two = lax.dot_general(matrix, matrix, NT, preferred_element_type=f32)
    divided = partial_two.reshape(Z, C, rows, -1)
    mine = lax.dynamic_index_in_dim(divided, index, 1, keepdims=False)
    other = lax.dynamic_index_in_dim(divided, 1 - index, 1, keepdims=False)
    mine = mine + lax.ppermute(other, "c", SWAP)
    tiles = mine.reshape(Z, X, rows // X, Y, -1).transpose(0, 1, 3, 2, 4)
    tile = exchange(tiles.reshape((Z * X * Y,) + tiles.shape[3:]), ("z", "x", "y")).sum(0)
    tile = tile / (variables * depth * X * Y * rank)
    second = to_all(tile, ("x", "y"), X * Y).reshape((X, Y) + tile.shape)
    return (factor_one, second.transpose(0, 2, 1, 3).reshape(rows, -1))


def solution(mesh):
    fine = Mesh(mesh.devices.reshape(Z, C, X, Y), ("z", "c", "x", "y"))
    placed = (P(None, ("x", "y"), ("z", "c"), None), P())
    return jax.shard_map(
        per_device, mesh=fine, in_specs=placed, out_specs=(P(), P(("z", "c"), None)), check_vma=False
    )
```

```python
import functools

import jax
import jax.numpy as jnp
from jax import lax
from jax.experimental import pallas as pl
from jax.experimental.pallas import tpu as pltpu
from jax.sharding import Mesh, PartitionSpec as P

ITERS = 6
Z, C, X, Y = 8, 2, 4, 4
B = 128
SWAP = [(0, 1), (1, 0)]
TN = (((0,), (0,)), ((), ()))
NT = (((1,), (1,)), ((), ()))
f32, bf16 = jnp.float32, jnp.bfloat16
vmem = pl.BlockSpec(memory_space=pltpu.VMEM)
smem = pl.BlockSpec(memory_space=pltpu.SMEM)
hbm = pl.BlockSpec(memory_space=pltpu.HBM)


def upper_pairs(tiles):
    return [(a, b) for a in range(tiles) for b in range(a, tiles)]


def gram_kernel(chunks, core_ref, x_hbm, mine_ref, other_ref, x_ref, upper, lower, sems):
    starts = [sum(chunks[:i]) for i in range(len(chunks))]
    copies = [
        pltpu.make_async_copy(x_hbm.at[pl.ds(at, size)], x_ref.at[pl.ds(at, size)], sems.at[i])
        for i, (at, size) in enumerate(zip(starts, chunks))
    ]
    for copy in copies:
        copy.start()
    h = lower.shape[0]
    for i, (at, size) in enumerate(zip(starts, chunks)):
        copies[i].wait()
        x = x_ref[pl.ds(at, size)]
        one = lax.dot_general(x[:, :h], x, TN, preferred_element_type=f32)
        two = lax.dot_general(x[:, h:], x[:, h:], TN, preferred_element_type=f32)
        if i:
            one, two = one + upper[...], two + lower[...]
        upper[...], lower[...] = one, two

    pairs = upper_pairs(upper.shape[1] // B)
    half = len(pairs) // 2

    def write(first_ref, last_ref):
        for place, (a, b) in enumerate(pairs):
            ref = first_ref if place < half else last_ref
            if a * B < h:
                block = upper[a * B:(a + 1) * B, b * B:(b + 1) * B]
            else:
                block = lower[a * B - h:(a + 1) * B - h, b * B - h:(b + 1) * B - h]
            ref[place % half] = block

    pl.when(core_ref[0] == 0)(lambda: write(mine_ref, other_ref))
    pl.when(core_ref[0] == 1)(lambda: write(other_ref, mine_ref))


def partial_gram(core, x):
    total, n = x.shape
    half = len(upper_pairs(n // B)) // 2
    out = jax.ShapeDtypeStruct((half, B, B), f32)
    chunks = (total // 11 * 3, total // 11 * 4, total // 11 * 4)
    return pl.pallas_call(
        functools.partial(gram_kernel, chunks),
        in_specs=[smem, hbm],
        out_specs=(vmem, vmem),
        out_shape=(out, out),
        scratch_shapes=[
            pltpu.VMEM((total, n), bf16),
            pltpu.VMEM((n // 2, n), f32),
            pltpu.VMEM((n // 2, n // 2), f32),
            pltpu.SemaphoreType.DMA((len(chunks),)),
        ],
        compiler_params=pltpu.CompilerParams(vmem_limit_bytes=50 * 2**20),
        name="partial_gram",
    )(core, x)


def split3(x):
    high = x.astype(bf16)
    rest = x - high.astype(f32)
    mid = rest.astype(bf16)
    return high, mid, (rest - mid.astype(f32)).astype(bf16)


def dot(a, b):
    return jnp.dot(a, b, preferred_element_type=f32)


def product(left, right):
    n = left[0].shape[0]
    one = dot(jnp.concatenate(left, 0), right[0])
    two = dot(jnp.concatenate(left[:2], 0), right[1])
    three = dot(left[0], right[2])
    return one[:n] + (one[n:2 * n] + two[:n] + (one[2 * n:] + two[n:] + three))


def pivots_beside_identity(parts):
    n = parts[0].shape[0]
    wide = [jnp.concatenate([part, jnp.zeros_like(part)], 0) for part in parts]

    def against(left, right):
        return lax.dot_general(jnp.concatenate(left, 0), right, NT, preferred_element_type=f32)

    one, two, three = against(parts, wide[0]), against(parts[:2], wide[1]), against(parts[:1], wide[2])
    total = one[:n] + ((one[n:2 * n] + two[:n]) + (two[n:] + (one[2 * n:] + three)))
    row = lax.broadcasted_iota(jnp.int32, (n, 2 * n), 0)
    lane = lax.broadcasted_iota(jnp.int32, (n, 2 * n), 1)
    return jnp.where(lane == row + n, 1.0, total)


def reciprocal(d):
    r = pl.reciprocal(d, approx=True)
    return r * (2.0 - d * r)


def inverse_factor(work):
    finished, pivots = [], []
    start = 0
    for panel in (16,) * 4:
        here = lax.broadcasted_iota(jnp.int32, work.shape, 0)
        columns = [
            jnp.broadcast_to(work[:, start + c:start + c + 1], work.shape) for c in range(panel)
        ]
        for j in range(0, panel, 2):
            u, v = columns[j], columns[j + 1]
            p, q, r = u[j:j + 1], u[j + 1:j + 2], v[j + 1:j + 2]
            over = reciprocal(p * r - q * q)
            below = here > j + 1
            one = jnp.where(below, (r * u - q * v) * over, 0.0)
            two = jnp.where(below, (p * v - q * u) * over, 0.0)
            for c in range(j + 2, panel):
                column = columns[c]
                columns[c] = column - (one * column[j:j + 1] + two * column[j + 1:j + 2])
            ratio = q * reciprocal(p)
            pivots += [p, r - q * ratio]
            one = jnp.where(here == j + 1, ratio, one)
            work = work - (one * work[j:j + 1] + two * work[j + 1:j + 2])
        finished.append(work[:panel])
        work = work[panel:]
        start += panel
    scale = lax.rsqrt(jnp.concatenate(pivots, 0))
    return jnp.concatenate(finished, 0) * scale


def orthonormal(images):
    parts = split3(images)
    inverse = inverse_factor(pivots_beside_identity(parts))
    below = tuple(jnp.concatenate([jnp.zeros_like(part), part], 0) for part in parts)
    return product(split3(inverse), below)


def factor_kernel(core_ref, x_hbm, mine_ref, other_ref, start_ref, factor_ref, shrunk_ref, g1, g2, g3, x_ref, sem):
    copy = pltpu.make_async_copy(x_hbm, x_ref, sem)
    copy.start()
    pairs = upper_pairs(g1.shape[0] // B)
    half = len(pairs) // 2
    even = core_ref[0] == 0
    unit = lax.broadcasted_iota(jnp.int32, (B, B), 0) == lax.broadcasted_iota(jnp.int32, (B, B), 1)

    def packed(place):
        mine, other = mine_ref[place % half], other_ref[place % half]
        return jnp.where(even, mine, other) if place < half else jnp.where(even, other, mine)

    diagonal = sum(jnp.where(unit, packed(place), 0.0) for place, (a, b) in enumerate(pairs) if a == b)
    over_trace = 1.0 / jnp.sum(diagonal, keepdims=True)
    for place, (a, b) in enumerate(pairs):
        block = packed(place) * over_trace
        for i, j in ((a, b), (b, a))[:1 if a == b else 2]:
            for ref, part in zip((g1, g2, g3), split3(block if i == a else block.T)):
                ref[i * B:(i + 1) * B, j * B:(j + 1) * B] = part

    def times_gram(parts):
        return product(parts, (g1[...], g2[...], g3[...]))

    def iteration(_, images):
        return times_gram(split3(orthonormal(images)))

    images = lax.fori_loop(0, ITERS - 1, iteration, times_gram(split3(start_ref[...])))
    factor = orthonormal(images)
    factor_ref[...] = factor

    narrow = factor.T.astype(bf16)
    n, rank = narrow.shape
    blank = jnp.zeros_like(narrow)
    both = jnp.concatenate(
        [jnp.concatenate([narrow, blank], 1), jnp.concatenate([blank, narrow], 1)], 0
    )
    variables, depth, rows, _ = x_ref.shape
    chunk, half_rows = depth // 2, rows // 2
    copy.wait()

    def shrink(t, _):
        k = pl.ds(t * chunk, chunk)

        def pair(left, right, at, size):
            x = jnp.concatenate([left.reshape(-1, n), right.reshape(-1, n)], 1)
            shrunk_ref[k, at:at + size, :] = dot(x, both).astype(bf16).reshape(chunk, size, 2 * rank)

        for v in range(0, variables - 1, 2):
            pair(x_ref[v, k], x_ref[v + 1, k], v // 2 * rows, rows)
        last = x_ref[variables - 1, k]
        pair(last[:, :half_rows], last[:, half_rows:], variables // 2 * rows, half_rows)
        return 0

    lax.fori_loop(0, depth // chunk, shrink, 0)


def factor_and_shrink(core, x, mine, other, start_factor):
    n, rank = start_factor.shape
    variables, depth, rows, _ = x.shape
    factor, shrunk = pl.pallas_call(
        factor_kernel,
        in_specs=[smem, hbm, vmem, vmem, vmem],
        out_specs=(vmem, vmem),
        out_shape=(
            jax.ShapeDtypeStruct((rank, n), f32),
            jax.ShapeDtypeStruct((depth, variables * rows // 2, 2 * rank), bf16),
        ),
        scratch_shapes=[pltpu.VMEM((n, n), bf16)] * 3
        + [pltpu.VMEM(x.shape, bf16), pltpu.SemaphoreType.DMA(())],
        compiler_params=pltpu.CompilerParams(vmem_limit_bytes=50 * 2**20),
        name="factor_and_shrink",
    )(core, x, mine, other, start_factor.T)
    return factor.T, shrunk


def rows_gram_kernel(core_ref, s_ref, mine_ref, other_ref, full):
    groups, length, width = s_ref.shape
    rank = width // 2
    rows = full.shape[0] // groups
    pairs = length // rows
    last = s_ref[:, pairs * rows:, :]
    left = lax.broadcasted_iota(jnp.int32, last.shape, 2) < rank
    swapped = jnp.concatenate([last[:, :, rank:], last[:, :, :rank]], 2)
    last = jnp.concatenate([jnp.where(left, last, 0), jnp.where(left, swapped, 0)], 1)
    blocks = [s_ref[:, p * rows:(p + 1) * rows, :] for p in range(pairs)] + [last]
    matrix = jnp.concatenate([block.reshape(-1, width) for block in blocks], 1)
    full[...] = lax.dot_general(matrix, matrix, NT, preferred_element_type=f32)
    core = core_ref[0]
    high = rows // X
    for ref, parity in ((other_ref, 1 - core), (mine_ref, core)):
        for z in range(groups // 2):
            for x in range(X):
                at = pl.multiple_of((2 * z + parity) * rows + x * high, 8)
                for y in range(full.shape[1] // B):
                    ref[x * Y + y, z] = full[pl.ds(at, high), y * B:(y + 1) * B]


def rows_gram(core, shrunk, rows):
    groups = shrunk.shape[0]
    n = groups * rows
    out = jax.ShapeDtypeStruct((X * Y, groups // 2, rows // X, n // Y), f32)
    return pl.pallas_call(
        rows_gram_kernel,
        in_specs=[smem, vmem],
        out_specs=(vmem, vmem),
        out_shape=(out, out),
        scratch_shapes=[pltpu.VMEM((n, n), f32)],
        compiler_params=pltpu.CompilerParams(vmem_limit_bytes=32 * 2**20),
        name="rows_gram",
    )(core, shrunk)


def exchange(pieces, axes):
    return lax.all_to_all(pieces, axes, 0, 0)


def to_all(piece, axes, count):
    return exchange(jnp.broadcast_to(piece[None], (count,) + piece.shape), axes)


def per_device(state_field, start_factor):
    variables, depth, rows, mode_one = state_field.shape
    rank = start_factor.shape[1]
    index = lax.axis_index("c")
    core = index.astype(jnp.int32)[None]

    mine, other = partial_gram(core, state_field.reshape(-1, mode_one))
    mine = mine + lax.ppermute(other, "c", SWAP)
    piece = exchange(mine.reshape(X * Y, -1, B), ("x", "y")).sum(0)
    piece = to_all(piece, "z", Z).sum(0)
    mine = to_all(piece, ("x", "y"), X * Y).reshape(mine.shape)
    other = lax.ppermute(mine, "c", SWAP)

    factor_one, shrunk = factor_and_shrink(core, state_field, mine, other, start_factor)

    mine, other = rows_gram(core, exchange(shrunk, ("z", "c")), rows)
    mine = mine + lax.ppermute(other, "c", SWAP)
    scale = 1.0 / (variables * depth * X * Y * rank)
    piece = exchange(mine, ("x", "y")).sum(0)
    tile = exchange(piece, "z").sum(0) * scale
    second = to_all(tile, ("x", "y"), X * Y).reshape((X, Y) + tile.shape)
    return (factor_one, second.transpose(0, 2, 1, 3).reshape(rows, -1))


def solution(mesh):
    fine = Mesh(mesh.devices.reshape(Z, C, X, Y), ("z", "c", "x", "y"))
    placed = (P(None, ("x", "y"), ("z", "c"), None), P())
    return jax.shard_map(
        per_device, mesh=fine, in_specs=placed, out_specs=(P(), P(("z", "c"), None)), check_vma=False
    )
```

```python
import functools

import jax
import jax.numpy as jnp
from jax import lax
from jax.experimental import pallas as pl
from jax.experimental.pallas import tpu as pltpu
from jax.sharding import Mesh, PartitionSpec as P

ITERS = 6
Z, C, X, Y = 8, 2, 4, 4
B = 128
SWAP = [(0, 1), (1, 0)]
TN = (((0,), (0,)), ((), ()))
NT = (((1,), (1,)), ((), ()))
f32, bf16 = jnp.float32, jnp.bfloat16
vmem = pl.BlockSpec(memory_space=pltpu.VMEM)
smem = pl.BlockSpec(memory_space=pltpu.SMEM)
hbm = pl.BlockSpec(memory_space=pltpu.HBM)


def upper_pairs(tiles):
    return [(a, b) for a in range(tiles) for b in range(a, tiles)]


def gram_kernel(chunks, core_ref, x_hbm, mine_ref, other_ref, x_ref, upper, lower, sems):
    starts = [sum(chunks[:i]) for i in range(len(chunks))]
    copies = [
        pltpu.make_async_copy(x_hbm.at[pl.ds(at, size)], x_ref.at[pl.ds(at, size)], sems.at[i])
        for i, (at, size) in enumerate(zip(starts, chunks))
    ]
    for copy in copies:
        copy.start()
    h = lower.shape[0]
    for i, (at, size) in enumerate(zip(starts, chunks)):

        @pl.when(core_ref[0] >= 0)
        def _():
            copies[i].wait()
            x = x_ref[pl.ds(at, size)]
            one = lax.dot_general(x[:, :h], x, TN, preferred_element_type=f32)
            two = lax.dot_general(x[:, h:], x[:, h:], TN, preferred_element_type=f32)
            if i:
                one, two = one + upper[...], two + lower[...]
            upper[...], lower[...] = one, two

    pairs = upper_pairs(upper.shape[1] // B)
    half = len(pairs) // 2

    def write(first_ref, last_ref):
        for place, (a, b) in enumerate(pairs):
            ref = first_ref if place < half else last_ref
            if a * B < h:
                block = upper[a * B:(a + 1) * B, b * B:(b + 1) * B]
            else:
                block = lower[a * B - h:(a + 1) * B - h, b * B - h:(b + 1) * B - h]
            ref[place % half] = block

    pl.when(core_ref[0] == 0)(lambda: write(mine_ref, other_ref))
    pl.when(core_ref[0] == 1)(lambda: write(other_ref, mine_ref))


def partial_gram(core, x):
    total, n = x.shape
    half = len(upper_pairs(n // B)) // 2
    out = jax.ShapeDtypeStruct((half, B, B), f32)
    chunks = (total // 11 * 2, total // 11 * 3, total // 11 * 6)
    return pl.pallas_call(
        functools.partial(gram_kernel, chunks),
        in_specs=[smem, hbm],
        out_specs=(vmem, vmem),
        out_shape=(out, out),
        scratch_shapes=[
            pltpu.VMEM((total, n), bf16),
            pltpu.VMEM((n // 2, n), f32),
            pltpu.VMEM((n // 2, n // 2), f32),
            pltpu.SemaphoreType.DMA((len(chunks),)),
        ],
        compiler_params=pltpu.CompilerParams(vmem_limit_bytes=50 * 2**20),
        name="partial_gram",
    )(core, x)


def split3(x):
    high = x.astype(bf16)
    rest = x - high.astype(f32)
    mid = rest.astype(bf16)
    return high, mid, (rest - mid.astype(f32)).astype(bf16)


def dot(a, b):
    return jnp.dot(a, b, preferred_element_type=f32)


def product(left, right):
    n = left[0].shape[0]
    one = dot(jnp.concatenate(left, 0), right[0])
    two = dot(jnp.concatenate(left[:2], 0), right[1])
    three = dot(left[0], right[2])
    return one[:n] + (one[n:2 * n] + two[:n] + (one[2 * n:] + two[n:] + three))


def pivots_beside_identity(parts):
    n = parts[0].shape[0]
    wide = [jnp.concatenate([part, jnp.zeros_like(part)], 0) for part in parts]

    def against(left, right):
        return lax.dot_general(jnp.concatenate(left, 0), right, NT, preferred_element_type=f32)

    one, two, three = against(parts, wide[0]), against(parts[:2], wide[1]), against(parts[:1], wide[2])
    total = one[:n] + ((one[n:2 * n] + two[:n]) + (two[n:] + (one[2 * n:] + three)))
    row = lax.broadcasted_iota(jnp.int32, (n, 2 * n), 0)
    lane = lax.broadcasted_iota(jnp.int32, (n, 2 * n), 1)
    return jnp.where(lane == row + n, 1.0, total)


def reciprocal(d):
    r = pl.reciprocal(d, approx=True)
    return r * (2.0 - d * r)


def inverse_factor(work):
    finished, pivots = [], []
    start = 0
    for panel in (16,) * 4:
        here = lax.broadcasted_iota(jnp.int32, work.shape, 0)
        columns = [
            jnp.broadcast_to(work[:, start + c:start + c + 1], work.shape) for c in range(panel)
        ]
        for j in range(0, panel, 2):
            u, v = columns[j], columns[j + 1]
            p, q, r = u[j:j + 1], u[j + 1:j + 2], v[j + 1:j + 2]
            over = reciprocal(p * r - q * q)
            below = here > j + 1
            one = jnp.where(below, (r * u - q * v) * over, 0.0)
            two = jnp.where(below, (p * v - q * u) * over, 0.0)
            for c in range(j + 2, panel):
                column = columns[c]
                columns[c] = column - (one * column[j:j + 1] + two * column[j + 1:j + 2])
            ratio = q * reciprocal(p)
            pivots += [p, r - q * ratio]
            one = jnp.where(here == j + 1, ratio, one)
            work = work - (one * work[j:j + 1] + two * work[j + 1:j + 2])
        finished.append(work[:panel])
        work = work[panel:]
        start += panel
    scale = lax.rsqrt(jnp.concatenate(pivots, 0))
    return jnp.concatenate(finished, 0) * scale


def orthonormal(images):
    parts = split3(images)
    inverse = inverse_factor(pivots_beside_identity(parts))
    below = tuple(jnp.concatenate([jnp.zeros_like(part), part], 0) for part in parts)
    return product(split3(inverse), below)


def factor_kernel(core_ref, x_hbm, mine_ref, other_ref, start_ref, factor_ref, shrunk_ref, g1, g2, g3, x_ref, sem):
    copy = pltpu.make_async_copy(x_hbm, x_ref, sem)
    copy.start()
    pairs = upper_pairs(g1.shape[0] // B)
    half = len(pairs) // 2
    even = core_ref[0] == 0
    unit = lax.broadcasted_iota(jnp.int32, (B, B), 0) == lax.broadcasted_iota(jnp.int32, (B, B), 1)

    def packed(place):
        mine, other = mine_ref[place % half], other_ref[place % half]
        return jnp.where(even, mine, other) if place < half else jnp.where(even, other, mine)

    diagonal = sum(jnp.where(unit, packed(place), 0.0) for place, (a, b) in enumerate(pairs) if a == b)
    over_trace = 1.0 / jnp.sum(diagonal, keepdims=True)
    for place, (a, b) in enumerate(pairs):
        block = packed(place) * over_trace
        for i, j in ((a, b), (b, a))[:1 if a == b else 2]:
            for ref, part in zip((g1, g2, g3), split3(block if i == a else block.T)):
                ref[i * B:(i + 1) * B, j * B:(j + 1) * B] = part

    def times_gram(parts):
        return product(parts, (g1[...], g2[...], g3[...]))

    def iteration(_, images):
        return times_gram(split3(orthonormal(images)))

    images = lax.fori_loop(0, ITERS - 1, iteration, times_gram(split3(start_ref[...])))
    factor = orthonormal(images)
    factor_ref[...] = factor

    narrow = factor.T.astype(bf16)
    n, rank = narrow.shape
    blank = jnp.zeros_like(narrow)
    both = jnp.concatenate(
        [jnp.concatenate([narrow, blank], 1), jnp.concatenate([blank, narrow], 1)], 0
    )
    variables, depth, rows, _ = x_ref.shape
    chunk, half_rows = depth // 2, rows // 2
    copy.wait()

    def shrink(t, _):
        k = pl.ds(t * chunk, chunk)

        def pair(left, right, at, size):
            x = jnp.concatenate([left.reshape(-1, n), right.reshape(-1, n)], 1)
            shrunk_ref[k, at:at + size, :] = dot(x, both).astype(bf16).reshape(chunk, size, 2 * rank)

        for v in range(0, variables - 1, 2):
            pair(x_ref[v, k], x_ref[v + 1, k], v // 2 * rows, rows)
        last = x_ref[variables - 1, k]
        pair(last[:, :half_rows], last[:, half_rows:], variables // 2 * rows, half_rows)
        return 0

    lax.fori_loop(0, depth // chunk, shrink, 0)


def factor_and_shrink(core, x, mine, other, start_factor):
    n, rank = start_factor.shape
    variables, depth, rows, _ = x.shape
    factor, shrunk = pl.pallas_call(
        factor_kernel,
        in_specs=[smem, hbm, vmem, vmem, vmem],
        out_specs=(vmem, vmem),
        out_shape=(
            jax.ShapeDtypeStruct((rank, n), f32),
            jax.ShapeDtypeStruct((depth, variables * rows // 2, 2 * rank), bf16),
        ),
        scratch_shapes=[pltpu.VMEM((n, n), bf16)] * 3
        + [pltpu.VMEM(x.shape, bf16), pltpu.SemaphoreType.DMA(())],
        compiler_params=pltpu.CompilerParams(vmem_limit_bytes=50 * 2**20),
        name="factor_and_shrink",
    )(core, x, mine, other, start_factor.T)
    return factor.T, shrunk


def rows_gram_kernel(core_ref, s_ref, mine_ref, other_ref, full):
    groups, length, width = s_ref.shape
    rank = width // 2
    rows = full.shape[0] // groups
    pairs = length // rows
    last = s_ref[:, pairs * rows:, :]
    left = lax.broadcasted_iota(jnp.int32, last.shape, 2) < rank
    swapped = jnp.concatenate([last[:, :, rank:], last[:, :, :rank]], 2)
    last = jnp.concatenate([jnp.where(left, last, 0), jnp.where(left, swapped, 0)], 1)
    blocks = [s_ref[:, p * rows:(p + 1) * rows, :] for p in range(pairs)] + [last]
    matrix = jnp.concatenate([block.reshape(-1, width) for block in blocks], 1)
    full[...] = lax.dot_general(matrix, matrix, NT, preferred_element_type=f32)
    core = core_ref[0]
    high = rows // X
    for ref, parity in ((other_ref, 1 - core), (mine_ref, core)):
        for z in range(groups // 2):
            for x in range(X):
                at = pl.multiple_of((2 * z + parity) * rows + x * high, 8)
                for y in range(full.shape[1] // B):
                    ref[x * Y + y, z] = full[pl.ds(at, high), y * B:(y + 1) * B]


def rows_gram(core, shrunk, rows):
    groups = shrunk.shape[0]
    n = groups * rows
    out = jax.ShapeDtypeStruct((X * Y, groups // 2, rows // X, n // Y), f32)
    return pl.pallas_call(
        rows_gram_kernel,
        in_specs=[smem, vmem],
        out_specs=(vmem, vmem),
        out_shape=(out, out),
        scratch_shapes=[pltpu.VMEM((n, n), f32)],
        compiler_params=pltpu.CompilerParams(vmem_limit_bytes=32 * 2**20),
        name="rows_gram",
    )(core, shrunk)


def exchange(pieces, axes):
    return lax.all_to_all(pieces, axes, 0, 0)


def to_all(piece, axes, count):
    return exchange(jnp.broadcast_to(piece[None], (count,) + piece.shape), axes)


def per_device(state_field, start_factor):
    variables, depth, rows, mode_one = state_field.shape
    rank = start_factor.shape[1]
    index = lax.axis_index("c")
    core = index.astype(jnp.int32)[None]

    mine, other = partial_gram(core, state_field.reshape(-1, mode_one))
    mine = mine + lax.ppermute(other, "c", SWAP)
    piece = exchange(mine.reshape(X * Y, -1, B), ("x", "y")).sum(0)
    piece = to_all(piece, "z", Z).sum(0)
    mine = to_all(piece, ("x", "y"), X * Y).reshape(mine.shape)
    other = lax.ppermute(mine, "c", SWAP)

    factor_one, shrunk = factor_and_shrink(core, state_field, mine, other, start_factor)

    mine, other = rows_gram(core, exchange(shrunk, ("z", "c")), rows)
    mine = mine + lax.ppermute(other, "c", SWAP)
    scale = 1.0 / (variables * depth * X * Y * rank)
    piece = exchange(mine, ("x", "y")).sum(0)
    tile = exchange(piece, "z").sum(0) * scale
    second = to_all(tile, ("x", "y"), X * Y).reshape((X, Y) + tile.shape)
    return (factor_one, second.transpose(0, 2, 1, 3).reshape(rows, -1))


def solution(mesh):
    fine = Mesh(mesh.devices.reshape(Z, C, X, Y), ("z", "c", "x", "y"))
    placed = (P(None, ("x", "y"), ("z", "c"), None), P())
    return jax.shard_map(
        per_device, mesh=fine, in_specs=placed, out_specs=(P(), P(("z", "c"), None)), check_vma=False
    )
```

```python
import functools

import jax
import jax.numpy as jnp
from jax import lax
from jax.experimental import pallas as pl
from jax.experimental.pallas import tpu as pltpu
from jax.sharding import Mesh, PartitionSpec as P

ITERS = 6
Z, C, X, Y = 8, 2, 4, 4
B = 128
SWAP = [(0, 1), (1, 0)]
TN = (((0,), (0,)), ((), ()))
NT = (((1,), (1,)), ((), ()))
f32, bf16 = jnp.float32, jnp.bfloat16
vmem = pl.BlockSpec(memory_space=pltpu.VMEM)
smem = pl.BlockSpec(memory_space=pltpu.SMEM)
hbm = pl.BlockSpec(memory_space=pltpu.HBM)


def upper_pairs(tiles):
    return [(a, b) for a in range(tiles) for b in range(a, tiles)]


def gram_kernel(chunks, core_ref, x_hbm, mine_ref, other_ref, x_ref, upper, lower, sems):
    starts = [sum(chunks[:i]) for i in range(len(chunks))]
    copies = [
        pltpu.make_async_copy(x_hbm.at[pl.ds(at, size)], x_ref.at[pl.ds(at, size)], sems.at[i])
        for i, (at, size) in enumerate(zip(starts, chunks))
    ]
    for copy in copies:
        copy.start()
    h = lower.shape[0]
    for i, (at, size) in enumerate(zip(starts, chunks)):

        @pl.when(core_ref[0] >= 0)
        def _():
            copies[i].wait()
            x = x_ref[pl.ds(at, size)]
            one = lax.dot_general(x[:, :h], x, TN, preferred_element_type=f32)
            two = lax.dot_general(x[:, h:], x[:, h:], TN, preferred_element_type=f32)
            if i:
                one, two = one + upper[...], two + lower[...]
            upper[...], lower[...] = one, two

    pairs = upper_pairs(upper.shape[1] // B)
    half = len(pairs) // 2

    def write(first_ref, last_ref):
        for place, (a, b) in enumerate(pairs):
            ref = first_ref if place < half else last_ref
            if a * B < h:
                block = upper[a * B:(a + 1) * B, b * B:(b + 1) * B]
            else:
                block = lower[a * B - h:(a + 1) * B - h, b * B - h:(b + 1) * B - h]
            ref[place % half] = block

    pl.when(core_ref[0] == 0)(lambda: write(mine_ref, other_ref))
    pl.when(core_ref[0] == 1)(lambda: write(other_ref, mine_ref))


def partial_gram(core, x):
    total, n = x.shape
    half = len(upper_pairs(n // B)) // 2
    out = jax.ShapeDtypeStruct((half, B, B), f32)
    chunks = (total // 11 * 2, total // 11 * 3, total // 11 * 6)
    return pl.pallas_call(
        functools.partial(gram_kernel, chunks),
        in_specs=[smem, hbm],
        out_specs=(vmem, vmem),
        out_shape=(out, out),
        scratch_shapes=[
            pltpu.VMEM((total, n), bf16),
            pltpu.VMEM((n // 2, n), f32),
            pltpu.VMEM((n // 2, n // 2), f32),
            pltpu.SemaphoreType.DMA((len(chunks),)),
        ],
        compiler_params=pltpu.CompilerParams(vmem_limit_bytes=50 * 2**20),
        name="partial_gram",
    )(core, x)


def split3(x):
    high = x.astype(bf16)
    rest = x - high.astype(f32)
    mid = rest.astype(bf16)
    return high, mid, (rest - mid.astype(f32)).astype(bf16)


def dot(a, b):
    return jnp.dot(a, b, preferred_element_type=f32)


def product(left, right):
    n = left[0].shape[0]
    one = dot(jnp.concatenate(left, 0), right[0])
    two = dot(jnp.concatenate(left[:2], 0), right[1])
    three = dot(left[0], right[2])
    return one[:n] + (one[n:2 * n] + two[:n] + (one[2 * n:] + two[n:] + three))


def pivots_beside_identity(parts):
    n = parts[0].shape[0]
    wide = [jnp.concatenate([part, jnp.zeros_like(part)], 0) for part in parts]

    def against(left, right):
        return lax.dot_general(jnp.concatenate(left, 0), right, NT, preferred_element_type=f32)

    one, two, three = against(parts, wide[0]), against(parts[:2], wide[1]), against(parts[:1], wide[2])
    total = one[:n] + ((one[n:2 * n] + two[:n]) + (two[n:] + (one[2 * n:] + three)))
    row = lax.broadcasted_iota(jnp.int32, (n, 2 * n), 0)
    lane = lax.broadcasted_iota(jnp.int32, (n, 2 * n), 1)
    return jnp.where(lane == row + n, 1.0, total)


def reciprocal(d):
    r = pl.reciprocal(d, approx=True)
    return r * (2.0 - d * r)


def inverse_factor(work):
    finished, pivots = [], []
    start = 0
    for panel in (16,) * 4:
        here = lax.broadcasted_iota(jnp.int32, work.shape, 0)
        columns = [
            jnp.broadcast_to(work[:, start + c:start + c + 1], work.shape) for c in range(panel)
        ]
        for j in range(0, panel, 2):
            u, v = columns[j], columns[j + 1]
            p, q, r = u[j:j + 1], u[j + 1:j + 2], v[j + 1:j + 2]
            over = reciprocal(p * r - q * q)
            below = here > j + 1
            one = jnp.where(below, (r * u - q * v) * over, 0.0)
            two = jnp.where(below, (p * v - q * u) * over, 0.0)
            for c in range(j + 2, panel):
                column = columns[c]
                columns[c] = column - (one * column[j:j + 1] + two * column[j + 1:j + 2])
            ratio = q * reciprocal(p)
            pivots += [p, r - q * ratio]
            one = jnp.where(here == j + 1, ratio, one)
            work = work - (one * work[j:j + 1] + two * work[j + 1:j + 2])
        finished.append(work[:panel])
        work = work[panel:]
        start += panel
    scale = lax.rsqrt(jnp.concatenate(pivots, 0))
    return jnp.concatenate(finished, 0) * scale


def orthonormal(images):
    parts = split3(images)
    inverse = inverse_factor(pivots_beside_identity(parts))
    below = tuple(jnp.concatenate([jnp.zeros_like(part), part], 0) for part in parts)
    return product(split3(inverse), below)


def factor_kernel(core_ref, x_hbm, mine_ref, other_ref, start_ref, factor_ref, shrunk_ref, g1, g2, g3, x_ref, sem):
    copy = pltpu.make_async_copy(x_hbm, x_ref, sem)
    copy.start()
    pairs = upper_pairs(g1.shape[0] // B)
    half = len(pairs) // 2
    even = core_ref[0] == 0
    unit = lax.broadcasted_iota(jnp.int32, (B, B), 0) == lax.broadcasted_iota(jnp.int32, (B, B), 1)

    def packed(place):
        mine, other = mine_ref[place % half], other_ref[place % half]
        return jnp.where(even, mine, other) if place < half else jnp.where(even, other, mine)

    diagonal = sum(jnp.where(unit, packed(place), 0.0) for place, (a, b) in enumerate(pairs) if a == b)
    over_trace = 1.0 / jnp.sum(diagonal, keepdims=True)
    for place, (a, b) in enumerate(pairs):
        block = packed(place) * over_trace
        for i, j in ((a, b), (b, a))[:1 if a == b else 2]:
            for ref, part in zip((g1, g2, g3), split3(block if i == a else block.T)):
                ref[i * B:(i + 1) * B, j * B:(j + 1) * B] = part

    def times_gram(parts):
        return product(parts, (g1[...], g2[...], g3[...]))

    def iteration(_, images):
        return times_gram(split3(orthonormal(images)))

    images = lax.fori_loop(0, ITERS - 1, iteration, times_gram(split3(start_ref[...])))
    factor = orthonormal(images)
    factor_ref[...] = factor

    narrow = factor.T.astype(bf16)
    n, rank = narrow.shape
    blank = jnp.zeros_like(narrow)
    both = jnp.concatenate(
        [jnp.concatenate([narrow, blank], 1), jnp.concatenate([blank, narrow], 1)], 0
    )
    variables, depth, rows, _ = x_ref.shape
    chunk, half_rows = depth // 2, rows // 2
    copy.wait()

    def shrink(t, _):
        k = pl.ds(t * chunk, chunk)

        def pair(left, right, at, size):
            x = jnp.concatenate([left.reshape(-1, n), right.reshape(-1, n)], 1)
            shrunk_ref[k, at:at + size, :] = dot(x, both).astype(bf16).reshape(chunk, size, 2 * rank)

        for v in range(0, variables - 1, 2):
            pair(x_ref[v, k], x_ref[v + 1, k], v // 2 * rows, rows)
        last = x_ref[variables - 1, k]
        pair(last[:, :half_rows], last[:, half_rows:], variables // 2 * rows, half_rows)
        return 0

    lax.fori_loop(0, depth // chunk, shrink, 0)


def factor_and_shrink(core, x, mine, other, start_factor):
    n, rank = start_factor.shape
    variables, depth, rows, _ = x.shape
    factor, shrunk = pl.pallas_call(
        factor_kernel,
        in_specs=[smem, hbm, vmem, vmem, vmem],
        out_specs=(vmem, vmem),
        out_shape=(
            jax.ShapeDtypeStruct((rank, n), f32),
            jax.ShapeDtypeStruct((depth, variables * rows // 2, 2 * rank), bf16),
        ),
        scratch_shapes=[pltpu.VMEM((n, n), bf16)] * 3
        + [pltpu.VMEM(x.shape, bf16), pltpu.SemaphoreType.DMA(())],
        compiler_params=pltpu.CompilerParams(vmem_limit_bytes=50 * 2**20),
        name="factor_and_shrink",
    )(core, x, mine, other, start_factor.T)
    return factor.T, shrunk


def rows_gram_kernel(core_ref, s_ref, mine_ref, other_ref, full):
    groups, length, width = s_ref.shape
    rank = width // 2
    rows = full.shape[0] // groups
    pairs = length // rows
    last = s_ref[:, pairs * rows:, :]
    left = lax.broadcasted_iota(jnp.int32, last.shape, 2) < rank
    swapped = jnp.concatenate([last[:, :, rank:], last[:, :, :rank]], 2)
    last = jnp.concatenate([jnp.where(left, last, 0), jnp.where(left, swapped, 0)], 1)
    blocks = [s_ref[:, p * rows:(p + 1) * rows, :] for p in range(pairs)] + [last]
    matrix = jnp.concatenate([block.reshape(-1, width) for block in blocks], 1)
    full[...] = lax.dot_general(matrix, matrix, NT, preferred_element_type=f32)
    core = core_ref[0]
    high = rows // X
    for ref, parity in ((other_ref, 1 - core), (mine_ref, core)):
        for z in range(groups // 2):
            for x in range(X):
                at = pl.multiple_of((2 * z + parity) * rows + x * high, 8)
                for y in range(full.shape[1] // B):
                    ref[x * Y + y, z] = full[pl.ds(at, high), y * B:(y + 1) * B]


def rows_gram(core, shrunk, rows):
    groups = shrunk.shape[0]
    n = groups * rows
    out = jax.ShapeDtypeStruct((X * Y, groups // 2, rows // X, n // Y), f32)
    return pl.pallas_call(
        rows_gram_kernel,
        in_specs=[smem, vmem],
        out_specs=(vmem, vmem),
        out_shape=(out, out),
        scratch_shapes=[pltpu.VMEM((n, n), f32)],
        compiler_params=pltpu.CompilerParams(vmem_limit_bytes=32 * 2**20),
        name="rows_gram",
    )(core, shrunk)


def exchange(pieces, axes):
    return lax.all_to_all(pieces, axes, 0, 0)


def to_all(piece, axes, count):
    return exchange(jnp.broadcast_to(piece[None], (count,) + piece.shape), axes)


def per_device(state_field, start_factor):
    variables, depth, rows, mode_one = state_field.shape
    rank = start_factor.shape[1]
    index = lax.axis_index("c")
    core = index.astype(jnp.int32)[None]

    mine, other = partial_gram(core, state_field.reshape(-1, mode_one))
    mine = mine + lax.ppermute(other, "c", SWAP)
    piece = exchange(mine.reshape(X * Y, -1, B), ("y", "x")).sum(0)
    piece = to_all(piece, "z", Z).sum(0)
    mine = to_all(piece, ("y", "x"), X * Y).reshape(mine.shape)
    other = lax.ppermute(mine, "c", SWAP)

    factor_one, shrunk = factor_and_shrink(core, state_field, mine, other, start_factor)

    mine, other = rows_gram(core, exchange(shrunk, ("z", "c")), rows)
    mine = mine + lax.ppermute(other, "c", SWAP)
    scale = 1.0 / (variables * depth * X * Y * rank)
    piece = exchange(mine, ("y", "x")).sum(0)
    tile = exchange(piece, "z").sum(0) * scale
    second = to_all(tile, ("y", "x"), X * Y).reshape((X, Y) + tile.shape)
    return (factor_one, second.transpose(0, 2, 1, 3).reshape(rows, -1))


def solution(mesh):
    fine = Mesh(mesh.devices.reshape(Z, C, X, Y), ("z", "c", "x", "y"))
    placed = (P(None, ("x", "y"), ("z", "c"), None), P())
    return jax.shard_map(
        per_device, mesh=fine, in_specs=placed, out_specs=(P(), P(("z", "c"), None)), check_vma=False
    )
```

```python
import functools

import jax
import jax.numpy as jnp
from jax import lax
from jax.experimental import pallas as pl
from jax.experimental.pallas import tpu as pltpu
from jax.sharding import Mesh, PartitionSpec as P

ITERS = 6
Z, C, X, Y = 8, 2, 4, 4
B = 128
SWAP = [(0, 1), (1, 0)]
TN = (((0,), (0,)), ((), ()))
NT = (((1,), (1,)), ((), ()))
f32, bf16 = jnp.float32, jnp.bfloat16
vmem = pl.BlockSpec(memory_space=pltpu.VMEM)
smem = pl.BlockSpec(memory_space=pltpu.SMEM)
hbm = pl.BlockSpec(memory_space=pltpu.HBM)


def upper_pairs(tiles):
    return [(a, b) for a in range(tiles) for b in range(a, tiles)]


def gram_kernel(chunks, core_ref, x_hbm, mine_ref, other_ref, x_ref, upper, lower, sems):
    starts = [sum(chunks[:i]) for i in range(len(chunks))]
    copies = [
        pltpu.make_async_copy(x_hbm.at[pl.ds(at, size)], x_ref.at[pl.ds(at, size)], sems.at[i])
        for i, (at, size) in enumerate(zip(starts, chunks))
    ]
    for copy in copies:
        copy.start()
    h = lower.shape[0]
    for i, (at, size) in enumerate(zip(starts, chunks)):

        @pl.when(core_ref[0] >= 0)
        def _():
            copies[i].wait()
            x = x_ref[pl.ds(at, size)]
            one = lax.dot_general(x[:, :h], x, TN, preferred_element_type=f32)
            two = lax.dot_general(x[:, h:], x[:, h:], TN, preferred_element_type=f32)
            if i:
                one, two = one + upper[...], two + lower[...]
            upper[...], lower[...] = one, two

    pairs = upper_pairs(upper.shape[1] // B)
    half = len(pairs) // 2

    def write(first_ref, last_ref):
        for place, (a, b) in enumerate(pairs):
            ref = first_ref if place < half else last_ref
            if a * B < h:
                block = upper[a * B:(a + 1) * B, b * B:(b + 1) * B]
            else:
                block = lower[a * B - h:(a + 1) * B - h, b * B - h:(b + 1) * B - h]
            ref[place % half] = block

    pl.when(core_ref[0] == 0)(lambda: write(mine_ref, other_ref))
    pl.when(core_ref[0] == 1)(lambda: write(other_ref, mine_ref))


def partial_gram(core, x):
    total, n = x.shape
    half = len(upper_pairs(n // B)) // 2
    out = jax.ShapeDtypeStruct((half, B, B), f32)
    chunks = (total // 11 * 2, total // 11 * 3, total // 11 * 6)
    return pl.pallas_call(
        functools.partial(gram_kernel, chunks),
        in_specs=[smem, hbm],
        out_specs=(vmem, vmem),
        out_shape=(out, out),
        scratch_shapes=[
            pltpu.VMEM((total, n), bf16),
            pltpu.VMEM((n // 2, n), f32),
            pltpu.VMEM((n // 2, n // 2), f32),
            pltpu.SemaphoreType.DMA((len(chunks),)),
        ],
        compiler_params=pltpu.CompilerParams(vmem_limit_bytes=50 * 2**20),
        name="partial_gram",
    )(core, x)


def split3(x):
    high = x.astype(bf16)
    rest = x - high.astype(f32)
    mid = rest.astype(bf16)
    return high, mid, (rest - mid.astype(f32)).astype(bf16)


def dot(a, b):
    return jnp.dot(a, b, preferred_element_type=f32)


def product(left, right):
    n = left[0].shape[0]
    one = dot(jnp.concatenate(left, 0), right[0])
    two = dot(jnp.concatenate(left[:2], 0), right[1])
    three = dot(left[0], right[2])
    return one[:n] + (one[n:2 * n] + two[:n] + (one[2 * n:] + two[n:] + three))


def pivots_beside_identity(parts):
    n = parts[0].shape[0]
    wide = [jnp.concatenate([part, jnp.zeros_like(part)], 0) for part in parts]

    def against(left, right):
        return lax.dot_general(jnp.concatenate(left, 0), right, NT, preferred_element_type=f32)

    one, two, three = against(parts, wide[0]), against(parts[:2], wide[1]), against(parts[:1], wide[2])
    total = one[:n] + ((one[n:2 * n] + two[:n]) + (two[n:] + (one[2 * n:] + three)))
    row = lax.broadcasted_iota(jnp.int32, (n, 2 * n), 0)
    lane = lax.broadcasted_iota(jnp.int32, (n, 2 * n), 1)
    return jnp.where(lane == row + n, 1.0, total)


def reciprocal(d):
    r = pl.reciprocal(d, approx=True)
    return r * (2.0 - d * r)


def inverse_factor(work):
    finished, pivots = [], []
    start = 0
    for panel in (16,) * 4:
        here = lax.broadcasted_iota(jnp.int32, work.shape, 0)
        columns = [
            jnp.broadcast_to(work[:, start + c:start + c + 1], work.shape) for c in range(panel)
        ]
        for j in range(0, panel, 2):
            u, v = columns[j], columns[j + 1]
            p, q, r = u[j:j + 1], u[j + 1:j + 2], v[j + 1:j + 2]
            over = reciprocal(p * r - q * q)
            below = here > j + 1
            one = jnp.where(below, (r * u - q * v) * over, 0.0)
            two = jnp.where(below, (p * v - q * u) * over, 0.0)
            for c in range(j + 2, panel):
                column = columns[c]
                columns[c] = column - (one * column[j:j + 1] + two * column[j + 1:j + 2])
            ratio = q * reciprocal(p)
            pivots += [p, r - q * ratio]
            one = jnp.where(here == j + 1, ratio, one)
            work = work - (one * work[j:j + 1] + two * work[j + 1:j + 2])
        finished.append(work[:panel])
        work = work[panel:]
        start += panel
    scale = lax.rsqrt(jnp.concatenate(pivots, 0))
    return jnp.concatenate(finished, 0) * scale


def orthonormal(images):
    parts = split3(images)
    inverse = inverse_factor(pivots_beside_identity(parts))
    below = tuple(jnp.concatenate([jnp.zeros_like(part), part], 0) for part in parts)
    return product(split3(inverse), below)


def factor_kernel(core_ref, x_hbm, mine_ref, other_ref, start_ref, factor_ref, shrunk_ref, g1, g2, g3, x_ref, sem):
    copy = pltpu.make_async_copy(x_hbm, x_ref, sem)
    copy.start()
    pairs = upper_pairs(g1.shape[0] // B)
    half = len(pairs) // 2
    even = core_ref[0] == 0
    unit = lax.broadcasted_iota(jnp.int32, (B, B), 0) == lax.broadcasted_iota(jnp.int32, (B, B), 1)

    def packed(place):
        mine, other = mine_ref[place % half], other_ref[place % half]
        return jnp.where(even, mine, other) if place < half else jnp.where(even, other, mine)

    diagonal = sum(jnp.where(unit, packed(place), 0.0) for place, (a, b) in enumerate(pairs) if a == b)
    over_trace = 1.0 / jnp.sum(diagonal, keepdims=True)
    for place, (a, b) in enumerate(pairs):
        block = packed(place) * over_trace
        for i, j in ((a, b), (b, a))[:1 if a == b else 2]:
            for ref, part in zip((g1, g2, g3), split3(block if i == a else block.T)):
                ref[i * B:(i + 1) * B, j * B:(j + 1) * B] = part

    def times_gram(parts):
        return product(parts, (g1[...], g2[...], g3[...]))

    def iteration(_, images):
        return times_gram(split3(orthonormal(images)))

    images = lax.fori_loop(0, ITERS - 1, iteration, times_gram(split3(start_ref[...])))
    factor = orthonormal(images)
    factor_ref[...] = factor

    narrow = factor.T.astype(bf16)
    n, rank = narrow.shape
    blank = jnp.zeros_like(narrow)
    both = jnp.concatenate(
        [jnp.concatenate([narrow, blank], 1), jnp.concatenate([blank, narrow], 1)], 0
    )
    variables, depth, rows, _ = x_ref.shape
    chunk, half_rows = depth // 2, rows // 2
    copy.wait()

    def shrink(t, _):
        k = pl.ds(t * chunk, chunk)

        def pair(left, right, at, size):
            x = jnp.concatenate([left.reshape(-1, n), right.reshape(-1, n)], 1)
            shrunk_ref[k, at:at + size, :] = dot(x, both).astype(bf16).reshape(chunk, size, 2 * rank)

        for v in range(0, variables - 1, 2):
            pair(x_ref[v, k], x_ref[v + 1, k], v // 2 * rows, rows)
        last = x_ref[variables - 1, k]
        pair(last[:, :half_rows], last[:, half_rows:], variables // 2 * rows, half_rows)
        return 0

    lax.fori_loop(0, depth // chunk, shrink, 0)


def factor_and_shrink(core, x, mine, other, start_factor):
    n, rank = start_factor.shape
    variables, depth, rows, _ = x.shape
    factor, shrunk = pl.pallas_call(
        factor_kernel,
        in_specs=[smem, hbm, vmem, vmem, vmem],
        out_specs=(vmem, vmem),
        out_shape=(
            jax.ShapeDtypeStruct((rank, n), f32),
            jax.ShapeDtypeStruct((depth, variables * rows // 2, 2 * rank), bf16),
        ),
        scratch_shapes=[pltpu.VMEM((n, n), bf16)] * 3
        + [pltpu.VMEM(x.shape, bf16), pltpu.SemaphoreType.DMA(())],
        compiler_params=pltpu.CompilerParams(vmem_limit_bytes=50 * 2**20),
        name="factor_and_shrink",
    )(core, x, mine, other, start_factor.T)
    return factor.T, shrunk


def rows_gram_kernel(core_ref, s_ref, mine_ref, other_ref, full):
    groups, length, width = s_ref.shape
    rank = width // 2
    rows = full.shape[0] // groups
    pairs = length // rows
    order = [c * (groups // C) + z for z in range(groups // C) for c in range(C)]
    s = jnp.concatenate([s_ref[g:g + 1] for g in order], 0)
    last = s[:, pairs * rows:, :]
    left = lax.broadcasted_iota(jnp.int32, last.shape, 2) < rank
    swapped = jnp.concatenate([last[:, :, rank:], last[:, :, :rank]], 2)
    last = jnp.concatenate([jnp.where(left, last, 0), jnp.where(left, swapped, 0)], 1)
    blocks = [s[:, p * rows:(p + 1) * rows, :] for p in range(pairs)] + [last]
    matrix = jnp.concatenate([block.reshape(-1, width) for block in blocks], 1)
    full[...] = lax.dot_general(matrix, matrix, NT, preferred_element_type=f32)
    core = core_ref[0]
    high = rows // X
    for ref, parity in ((other_ref, 1 - core), (mine_ref, core)):
        for z in range(groups // 2):
            for x in range(X):
                at = pl.multiple_of((2 * z + parity) * rows + x * high, 8)
                for y in range(full.shape[1] // B):
                    ref[x * Y + y, z] = full[pl.ds(at, high), y * B:(y + 1) * B]


def rows_gram(core, shrunk, rows):
    groups = shrunk.shape[0]
    n = groups * rows
    out = jax.ShapeDtypeStruct((X * Y, groups // 2, rows // X, n // Y), f32)
    return pl.pallas_call(
        rows_gram_kernel,
        in_specs=[smem, vmem],
        out_specs=(vmem, vmem),
        out_shape=(out, out),
        scratch_shapes=[pltpu.VMEM((n, n), f32)],
        compiler_params=pltpu.CompilerParams(vmem_limit_bytes=32 * 2**20),
        name="rows_gram",
    )(core, shrunk)


def exchange(pieces, axes):
    return lax.all_to_all(pieces, axes, 0, 0)


def to_all(piece, axes, count):
    return exchange(jnp.broadcast_to(piece[None], (count,) + piece.shape), axes)


def per_device(state_field, start_factor):
    variables, depth, rows, mode_one = state_field.shape
    rank = start_factor.shape[1]
    index = lax.axis_index("c")
    core = index.astype(jnp.int32)[None]

    mine, other = partial_gram(core, state_field.reshape(-1, mode_one))
    mine = mine + lax.ppermute(other, "c", SWAP)
    piece = exchange(mine.reshape(X * Y, -1, B), ("y", "x")).sum(0)
    piece = to_all(piece, "z", Z).sum(0)
    mine = to_all(piece, ("y", "x"), X * Y).reshape(mine.shape)
    other = lax.ppermute(mine, "c", SWAP)

    factor_one, shrunk = factor_and_shrink(core, state_field, mine, other, start_factor)

    mine, other = rows_gram(core, exchange(shrunk, ("c", "z")), rows)
    mine = mine + lax.ppermute(other, "c", SWAP)
    scale = 1.0 / (variables * depth * X * Y * rank)
    piece = exchange(mine, ("y", "x")).sum(0)
    tile = exchange(piece, "z").sum(0) * scale
    second = to_all(tile, ("y", "x"), X * Y).reshape((X, Y) + tile.shape)
    return (factor_one, second.transpose(0, 2, 1, 3).reshape(rows, -1))


def solution(mesh):
    fine = Mesh(mesh.devices.reshape(Z, C, X, Y), ("z", "c", "x", "y"))
    placed = (P(None, ("x", "y"), ("z", "c"), None), P())
    return jax.shard_map(
        per_device, mesh=fine, in_specs=placed, out_specs=(P(), P(("z", "c"), None)), check_vma=False
    )
```
